256 devices in a mesh: seq: 64 (over z_lo, x, y), head: 4 (over z_hi, core).
Axes of the slice: x: 4, y: 4, z: 8 (z_hi: 2, z_lo: 4; z = z_hi * 4 + z_lo), core: 2. Of those that a mesh axis runs over, the one named last changes fastest.
Arguments:
- tokens: bfloat16 [131072, 1024], P('seq'), may hold values from -6 to 6
- norm_gain: float32 [1024], replicated, may hold values from 0.1 to 1.9
- w_qkv: bfloat16 [1024, 3, 1024], P(None, None, 'head'), may hold values from -10.5 to 10.5
- w_out: bfloat16 [1024, 1024], P('head'), may hold values from -0.75 to 0.75
Outputs:
- mixed: float32 [131072, 1024], P(('seq', 'head'))
The draws below stay inside these ranges and needn't reach their ends.
All inputs are finite; a program needn't handle non-finite values.
Results may differ from the reference program's by a relative error of at most 0.009.
The reference program's roundings to bfloat16 on the way count: a program that leaves them out, or rounds other values in their place, can miss the bound.
Values may be sent and summed in bfloat16 or wider, within the bound.
A program may use at most 128 MiB of HBM per device.

```python
import math
import jax
import jax.numpy as jnp
from jax import lax

D = 1024
HEADS = 16
HEAD_SIZE = 64
TOK_DEV = 2048
DILATION_MID = 8
DILATION_WHOLE = 64
SEGMENT_MID = 16384
TOKEN_COUNT = 131072
HEADS_DEV = 4
N_SEQ = 64
N_HEAD = 4


def draw_tokens(key, part):
    key = jax.random.fold_in(key, 5)
    key_base = jax.random.fold_in(key, 0)
    drawn = jnp.clip(jax.random.normal(key_base, (TOKEN_COUNT, D), jnp.float32), -6.0, 6.0)
    return drawn.astype(jnp.bfloat16)


def draw_w_qkv(key, part):
    key = jax.random.fold_in(key, 9)
    key_entries = jax.random.fold_in(key, 0)
    column_scale = jnp.array([math.sqrt(2.0 / D), math.sqrt(2.0 / D), math.sqrt(1.0 / D)], jnp.float32)
    entries = jnp.clip(jax.random.normal(key_entries, (D, 3, D), jnp.float32), -4.0, 4.0) * column_scale[None, :, None]
    return entries.astype(jnp.bfloat16)


def shard_levels(own_key, extent, pieces, smallest, top_value):
    factor_of = 1.0
    for position, shards_of in pieces:
        heights = jax.random.uniform(jax.random.fold_in(jax.random.fold_in(own_key, 6), position), (shards_of,), jnp.float32, smallest / len(pieces), top_value / len(pieces))
        factor_of = factor_of * jnp.repeat(jnp.exp(heights), extent[position] // shards_of).reshape((-1,) + (1,) * (len(extent) - 1 - position))
    return factor_of


def scatter_about(stream_key, dims, scale, bound, cuts=(), kind=jnp.bfloat16):
    level = shard_levels(stream_key, dims, cuts, -0.22, 0.18) if cuts else 1.0
    values = jax.random.normal(stream_key, dims, jnp.float32) * scale * level
    return jnp.minimum(jnp.maximum(values, -bound), bound).astype(kind)


def setup_inputs(seed: int = 0) -> dict:
    key_list = jax.random.split(jax.random.key(seed), 5)
    return {
        "tokens": draw_tokens(jax.random.fold_in(key_list[4], 71), 0),
        "norm_gain": jnp.clip(1.0 + 0.18 * jax.random.normal(key_list[1], (D,), jnp.float32), 0.1, 1.9),
        "w_qkv": draw_w_qkv(jax.random.fold_in(key_list[4], 71), 0),
        "w_out": scatter_about(key_list[3], (D, D), (D // 16) ** -0.5, 0.75, ((0, 4),)),
    }


norm_eps = 1e-05

def layer_norm(token_rows, norm_gain):
    widened = token_rows.astype(jnp.float32)
    center = lax.optimization_barrier(jnp.mean(widened, axis=-1, keepdims=True))
    variance = lax.optimization_barrier(jnp.mean((widened - center) ** 2, axis=-1, keepdims=True))
    return ((widened - center) * lax.rsqrt(variance + norm_eps) * norm_gain).astype(jnp.bfloat16)

def attend_heads(query_matrix, key_portion, value_portion):
    scores = jnp.dot(query_matrix, key_portion.T, preferred_element_type=jnp.float32) * key_portion.shape[-1] ** (-0.5)
    row_peak = lax.optimization_barrier(jnp.max(scores, axis=-1, keepdims=True))
    expanded = jnp.exp(scores - row_peak)
    row_total = lax.optimization_barrier(jnp.sum(expanded, axis=-1, keepdims=True))
    probabilities = (expanded / row_total).astype(jnp.bfloat16)
    result = jnp.dot(probabilities, value_portion, preferred_element_type=jnp.float32)
    return (result, row_peak[:, 0] + jnp.log(row_total[:, 0]))

def blend_branches(lse_one, out_one, logsumexp_second, output_second, logsumexp_third, output_third):
    highest = jnp.maximum(jnp.maximum(lse_one, logsumexp_second), logsumexp_third)
    weight_one = jnp.exp(lse_one - highest)[..., None]
    weight_two = jnp.exp(logsumexp_second - highest)[..., None]
    weight_three = jnp.exp(logsumexp_third - highest)[..., None]
    summed = weight_one * out_one + weight_two * output_second + weight_three * output_third
    return summed / (weight_one + weight_two + weight_three)

def attend_segments(query_matrix, key_portion, value_portion):
    return lax.map(lambda triple: attend_heads(triple[0], triple[1], triple[2]), (query_matrix, key_portion, value_portion))

def reference(tokens, norm_gain, w_qkv, w_out):
    flat_weight = w_qkv.reshape(D, 3 * D)

    def project(token_rows):
        return jnp.dot(layer_norm(token_rows, norm_gain), flat_weight, preferred_element_type=jnp.float32).astype(jnp.bfloat16)
    projected = lax.map(project, tokens.reshape(N_SEQ, TOK_DEV, D)).reshape(TOKEN_COUNT, 3, HEADS, HEAD_SIZE)
    head_outputs = []
    for head_number in range(HEADS):
        query_matrix = projected[:, 0, head_number]
        key_portion = projected[:, 1, head_number]
        value_portion = projected[:, 2, head_number]
        out_one, lse_one = attend_segments(query_matrix.reshape(N_SEQ, TOK_DEV, HEAD_SIZE), key_portion.reshape(N_SEQ, TOK_DEV, HEAD_SIZE), value_portion.reshape(N_SEQ, TOK_DEV, HEAD_SIZE))
        out_one = out_one.reshape(TOKEN_COUNT, HEAD_SIZE)
        lse_one = lse_one.reshape(TOKEN_COUNT)
        start_offset = head_number % DILATION_MID
        segment_total = TOKEN_COUNT // SEGMENT_MID
        segment_span_length = SEGMENT_MID // DILATION_MID
        output_second, logsumexp_second = attend_segments(query_matrix[start_offset::DILATION_MID].reshape(segment_total, segment_span_length, HEAD_SIZE), key_portion[start_offset::DILATION_MID].reshape(segment_total, segment_span_length, HEAD_SIZE), value_portion[start_offset::DILATION_MID].reshape(segment_total, segment_span_length, HEAD_SIZE))
        whole_output_second = jnp.zeros((TOKEN_COUNT, HEAD_SIZE), jnp.float32).at[start_offset::DILATION_MID].set(output_second.reshape(-1, HEAD_SIZE))
        whole_logsumexp_second = jnp.full((TOKEN_COUNT,), -1e+30, jnp.float32).at[start_offset::DILATION_MID].set(logsumexp_second.reshape(-1))
        distant_offset = head_number % DILATION_WHOLE
        output_third, logsumexp_third = attend_heads(query_matrix[distant_offset::DILATION_WHOLE], key_portion[distant_offset::DILATION_WHOLE], value_portion[distant_offset::DILATION_WHOLE])
        whole_output_third = jnp.zeros((TOKEN_COUNT, HEAD_SIZE), jnp.float32).at[distant_offset::DILATION_WHOLE].set(output_third)
        whole_logsumexp_third = jnp.full((TOKEN_COUNT,), -1e+30, jnp.float32).at[distant_offset::DILATION_WHOLE].set(logsumexp_third)
        blended = blend_branches(lse_one, out_one, whole_logsumexp_second, whole_output_second, whole_logsumexp_third, whole_output_third)
        head_outputs.append(blended.astype(jnp.bfloat16))
    attended = jnp.concatenate(head_outputs, axis=1)
    group_width = HEADS_DEV * HEAD_SIZE
    combined = jnp.zeros((TOKEN_COUNT, D), jnp.float32)
    for group_id in range(N_HEAD):
        lower = group_id * group_width
        partial_value = jnp.dot(attended[:, lower:lower + group_width], w_out[lower:lower + group_width], preferred_element_type=jnp.float32).astype(jnp.bfloat16)
        partial_value = lax.optimization_barrier(partial_value)
        combined = combined + partial_value.astype(jnp.float32)
    return combined
```

```python
import functools

import jax
import jax.numpy as jnp
from jax import lax
from jax.experimental import pallas as pl
from jax.experimental.pallas import tpu as pltpu
from jax.sharding import PartitionSpec as P

MESH = pl.DeviceIdType.MESH
F32 = jnp.float32
BF16 = jnp.bfloat16
EPS = 1e-05
LOG2E = 1.4426950408889634
HEADS = 4
HEAD = 64
ROWS = 512
FEATS = 256
KEYS = 2048
CHUNK = 256
NEG = -1e30

RELATION = (2, 3, 1, 0)

COPIES = (
    ["wc", "wz", "w2", "mq", "mp"]
    + [f"wy{i}" for i in (1, 2, 3)]
    + [f"wx{i}" for i in (1, 2, 3)]
    + [f"my{i}" for i in (1, 2, 3)]
    + [f"fz{i}" for i in (1, 2, 3)]
    + [f"fy{i}" for i in (1, 2, 3)]
    + [f"fq{i}" for i in (1, 2, 3)]
    + [f"fp{i}" for i in (1, 2, 3)]
    + [f"b{i}" for i in range(3)]
    + [f"f{i}" for i in range(3)]
)
SLOT = {name: i for i, name in enumerate(COPIES)}


def dot(a, b):
    return jnp.dot(a, b, preferred_element_type=F32)


def kernel(
    tokens_hbm, gain_ref, wqkv_hbm, wout_hbm, out_ref,
    tok, wq, normed, pp, kd, qt, vt, kvm, qm, qmp, vtm, kvff, kvf, qff, qf, qfp, vtf,
    pm_own, pm_st, pm_r, pf_st, pf_r, locacc, att_st, att_r, fx_st, fx_r, wo, s0, s1,
    send_sem, recv_sem, tok_sem, w_sem, wo_sem,
):
    seq = lax.axis_index("seq")
    g = lax.axis_index("head")
    zl, x, y = seq // 16, (seq // 4) % 4, seq % 4
    zhi, core = g // 2, g % 2

    def at_y(i):
        return (zl * 16 + x * 4 + (y + i) % 4, g)

    def at_x(i):
        return (zl * 16 + ((x + i) % 4) * 4 + y, g)

    def at_z(i):
        return (((zl + i) % 4) * 16 + x * 4 + y, g)

    x_pair = (zl * 16 + (x + 1 - 2 * (x % 2)) * 4 + y, g)

    def group(k):
        a, b = RELATION[k] // 2, RELATION[k] % 2
        return ((zhi + a) % 2) * 2 + (core + b) % 2

    def at_rel(k):
        return (seq, group(k))

    everyone = [at_y(i) for i in (1, 2, 3)] + [at_x(i) for i in (1, 2, 3)]
    everyone += [at_z(i) for i in (1, 2, 3)] + [at_rel(k) for k in (0, 1, 2)]
    barrier = pltpu.get_barrier_semaphore()
    for device in everyone:
        pl.semaphore_signal(barrier, inc=1, device_id=device, device_id_type=MESH)

    def copy(name):
        piece = pl.ds(pl.multiple_of(16 * (x * 4 + y), 16), 16)
        quarter = pl.ds(pl.multiple_of(64 * x, 64), 64)
        kind, i = name[:-1], name[-1]
        if name == "wc":
            src, dst, dev = wo.at[3], wo.at[2], at_rel(2)
        elif name == "wz":
            src, dst, dev = wo.at[3, piece], wo.at[0, piece], at_rel(0)
        elif name == "w2":
            src, dst, dev = wo.at[0], wo.at[1], at_rel(2)
        elif name == "mq":
            src, dst, dev = qm.at[0], qm.at[1], x_pair
        elif name == "mp":
            src, dst, dev = pm_st, pm_r, x_pair
        elif kind == "wy":
            src, dst, dev = wo.at[0, piece], wo.at[0, piece], at_y(int(i))
        elif kind == "wx":
            src, dst, dev = wo.at[0, quarter], wo.at[0, quarter], at_x(int(i))
        elif kind == "my":
            src, dst, dev = kvm.at[0], kvm.at[int(i)], at_y(int(i))
        elif kind == "fz":
            src, dst, dev = kvf.at[0, 0], kvf.at[0, int(i)], at_z(int(i))
        elif kind == "fy":
            src, dst, dev = kvf.at[0], kvf.at[int(i)], at_y(int(i))
        elif kind == "fq":
            src, dst, dev = qf.at[0], qf.at[int(i)], at_x(int(i))
        elif kind == "fp":
            src, dst, dev = pf_st.at[int(i)], pf_r.at[int(i) - 1], at_x(4 - int(i))
        elif kind == "b":
            src, dst, dev = att_st.at[int(i)], att_r.at[int(i)], at_rel(int(i))
        else:
            src, dst, dev = fx_st.at[int(i)], fx_r.at[int(i)], at_rel(int(i))
        return pltpu.make_async_remote_copy(
            src_ref=src, dst_ref=dst, send_sem=send_sem.at[SLOT[name]], recv_sem=recv_sem.at[SLOT[name]],
            device_id=dev, device_id_type=MESH,
        )

    def start(*names):
        for name in names:
            copy(name).start()

    def arrived(*names):
        for name in names:
            copy(name).wait_recv()

    def three(kind):
        return [f"{kind}{i}" for i in (1, 2, 3)]

    def tok_copy(k):
        rows = pl.ds(pl.multiple_of(group(k) * ROWS, ROWS), ROWS)
        return pltpu.make_async_copy(tokens_hbm.at[rows], tok.at[k], tok_sem.at[k])

    w_copies = [pltpu.make_async_copy(wqkv_hbm.at[i], wq.at[i], w_sem.at[i]) for i in range(3)]
    wo_copy = pltpu.make_async_copy(wout_hbm, wo.at[3], wo_sem)
    tok_copy(0).start()
    for c in w_copies:
        c.start()
    wo_copy.start()
    for k in (1, 2, 3):
        tok_copy(k).start()

    vt[:, HEAD:, :] = jnp.ones((HEADS, 16, KEYS), BF16)
    vtm[:, HEAD:, :] = jnp.ones((HEADS, 16, 1024), BF16)
    vtf[:, HEAD:, :] = jnp.ones((HEADS, 16, 512), BF16)
    qmp[:, HEAD:, :] = jnp.zeros((HEADS, HEAD, 512), BF16)
    qfp[:, HEAD:, :] = jnp.zeros((HEADS, HEAD, 128), BF16)

    odd = pl.multiple_of(256 * core, 256)

    def project(k):
        for part in range(16):
            rows = pl.ds(part * 32, 32)
            wide = tok[k, rows, :].astype(F32)
            center = jnp.mean(wide, axis=1, keepdims=True)
            wide = wide - center
            variance = jnp.mean(wide * wide, axis=1, keepdims=True)
            normed[rows, :] = (wide * lax.rsqrt(variance + EPS) * gain_ref[...]).astype(BF16)
        if k == 0:
            for c in w_copies:
                c.wait()
        for i in range(3):
            for half in range(2):
                result = dot(normed[half * 256:(half + 1) * 256, :], wq[i])
                for m in range(32):
                    b, c = half * 4 + m // 8, m % 8
                    for t in range(2):
                        pp[2 * i + t, pl.ds(8 * c + b, 8, stride=64), :] = result[8 * m:8 * m + 8, 128 * t:128 * t + 128]
        lanes = pl.ds(k * ROWS, ROWS)

        def piece(section, h, rows):
            return pp[2 * section + h // 2, rows, h % 2 * HEAD:h % 2 * HEAD + HEAD]

        for pair in range(2):
            queries = pp[pair].T.astype(BF16).astype(F32) * (0.125 * LOG2E)
            high = queries.astype(BF16)
            low = (queries - high.astype(F32)).astype(BF16)
            values = pp[4 + pair].T.astype(BF16)
            for side in range(2):
                feats = slice(side * HEAD, (side + 1) * HEAD)
                qt[2 * pair + side, :HEAD, lanes] = high[feats]
                qt[2 * pair + side, HEAD:, lanes] = low[feats]
                vt[2 * pair + side, :HEAD, lanes] = values[feats]
        for h in range(HEADS):
            feats = slice(h * HEAD, (h + 1) * HEAD)
            key = piece(1, h, slice(None))
            kd[h, lanes, :] = jnp.concatenate([key, key], axis=1).astype(BF16)
            mid_rows = pl.ds(odd + h * 64, 64)
            far_rows = pl.ds(pl.multiple_of(odd + h * 64 + 8 * zhi, 8), 8)
            pair = jnp.concatenate([piece(1, h, mid_rows), piece(2, h, mid_rows)], axis=1)
            kvm[0, h, k * 64:(k + 1) * 64, :] = pair.astype(BF16)
            qm[0, k * 64:(k + 1) * 64, feats] = piece(0, h, mid_rows).astype(BF16)
            kvff[h, k * 8:(k + 1) * 8, :] = jnp.concatenate([piece(1, h, far_rows), piece(2, h, far_rows)], axis=1)
            qff[k * 8:(k + 1) * 8, feats] = piece(0, h, far_rows)

    for k in range(4):
        tok_copy(k).wait()
        project(k)
        if k == 0:
            pl.semaphore_wait(barrier, len(everyone))
            wo_copy.wait()
            start("wc", "wz")
        if k == 2:
            arrived("wz")
            start(*three("wy"))
    kvf[0, 0] = kvff[...].astype(BF16)
    qf[0] = qff[...].astype(BF16)
    start(*three("fz"), "mq", *three("fq"), *three("my"))

    def top_rows(den8, m):
        row = lax.broadcasted_iota(jnp.int32, den8.shape, 0)
        return jnp.where(row == 0, den8, m)

    def scores(u, slot, c, peak):
        k, h = u // 4, u % 4
        lanes = pl.ds(pl.multiple_of(k * ROWS, ROWS), ROWS)
        s = dot(kd[h, c * CHUNK:(c + 1) * CHUNK, :], qt[h, :, lanes])
        slot[c * CHUNK:(c + 1) * CHUNK, :] = s
        t = jnp.max(s.reshape(CHUNK // 8, 8, ROWS), axis=0)
        return t if peak is None else jnp.maximum(peak, t)

    def weigh(u, slot, c, m, acc):
        h = u % 4
        p = jnp.exp2(slot[c * CHUNK:(c + 1) * CHUNK, :] - m).astype(BF16)
        o = dot(vt[h, :, c * CHUNK:(c + 1) * CHUNK], p)
        return o if acc is None else acc + o

    def finish(u, acc, m):
        k, h = u // 4, u % 4
        feats = pl.ds(pl.multiple_of(h * HEAD, HEAD), HEAD)
        att_st[k, feats, :] = (acc[:HEAD] * (1.0 / acc[HEAD:HEAD + 1])).astype(BF16)
        locacc[k, h, :HEAD, :] = acc[:HEAD]
        locacc[k, h, HEAD:, :] = top_rows(acc[HEAD:HEAD + 8], m)

    def half(u, cur, nxt, m, last=False):
        peak = acc = None
        for c in range(KEYS // CHUNK):
            if not last:
                peak = scores(u + 1, nxt, c, peak)
            acc = weigh(u, cur, c, m, acc)
        finish(u, acc, m)
        return None if last else jnp.max(peak, axis=0, keepdims=True)

    def local(first, final, steps):
        peak = None
        for c in range(KEYS // CHUNK):
            peak = scores(first, s0, c, peak)
        m = jnp.max(peak, axis=0, keepdims=True)

        def body(i, m):
            u = first + 2 * i
            m = half(u, s0, s1, m)
            m = half(u + 1, s1, s0, m)
            for at, step in steps.items():
                pl.when(i == at)(step)
            return m

        m = lax.fori_loop(0, (final - first) // 2 - 1, body, m)
        m = half(final - 2, s0, s1, m)
        half(final - 1, s1, s0, m, last=True)

    def step0():
        arrived(*three("fz"))
        start(*three("fy"))

    def step1():
        start("b0")
        arrived(*three("wy"))
        start(*three("wx"))

    def step3():
        start("b1")
        arrived(*three("wx"))
        start("w2")

    local(0, 12, {0: step0, 1: step1, 3: step3})
    start("b2")

    arrived("mq", *three("my"))
    for i in range(2):
        turned = (qm[i].astype(F32) * 0.125).T.astype(BF16)
        for h in range(HEADS):
            qmp[h, :HEAD, i * 256:(i + 1) * 256] = turned[h * HEAD:(h + 1) * HEAD]
    for i in range(4):
        for h in range(HEADS):
            vtm[h, :HEAD, i * 256:(i + 1) * 256] = kvm[i, h].astype(F32).T[HEAD:].astype(BF16)

    def mid_scores(h, slot, c, peak):
        s = dot(kvm[c, h], qmp[h]) * LOG2E
        slot[c * CHUNK:(c + 1) * CHUNK, :] = s
        t = jnp.max(s.reshape(CHUNK // 8, 8, 512), axis=0)
        return t if peak is None else jnp.maximum(peak, t)

    def mid_weigh(h, slot, c, m, acc):
        p = jnp.exp2(slot[c * CHUNK:(c + 1) * CHUNK, :] - m).astype(BF16)
        o = dot(vtm[h, :, c * CHUNK:(c + 1) * CHUNK], p)
        return o if acc is None else acc + o

    peak = None
    for c in range(4):
        peak = mid_scores(0, s0, c, peak)
    for h in range(HEADS):
        cur, nxt = (s0, s1) if h % 2 == 0 else (s1, s0)
        m = jnp.max(peak, axis=0, keepdims=True)
        peak = acc = None
        for c in range(4):
            if h < 3:
                peak = mid_scores(h + 1, nxt, c, peak)
            acc = mid_weigh(h, cur, c, m, acc)
        tail = top_rows(acc[HEAD:HEAD + 8], m)
        pm_st[h, :HEAD, :] = acc[:HEAD, 256:]
        pm_st[h, HEAD:, :] = tail[:, 256:]
        pm_own[h, :HEAD, :] = acc[:HEAD, :256]
        pm_own[h, HEAD:, :] = tail[:, :256]
    start("mp")

    arrived(*three("fy"), *three("fq"))
    gathered = jnp.concatenate([qf[i] for i in range(4)], axis=0)
    turned = (gathered.astype(F32) * 0.125).T.astype(BF16)
    far_parts = []
    for h in range(HEADS):
        qfp[h, :HEAD, :] = turned[h * HEAD:(h + 1) * HEAD]
        keyval = kvf[:, :, h].reshape(512, 128)
        vtf[h, :HEAD, :] = keyval.astype(F32).T[HEAD:].astype(BF16)
        s = dot(keyval, qfp[h]) * LOG2E
        m = jnp.max(s, axis=0, keepdims=True)
        p = jnp.exp2(s - m).astype(BF16)
        acc = dot(vtf[h], p)
        far_parts.append(jnp.concatenate([acc[:HEAD], top_rows(acc[HEAD:HEAD + 8], m)], axis=0))
    lane = lax.broadcasted_iota(jnp.int32, (72, 128), 1)
    for i in range(4):
        packed = None
        for h in range(HEADS):
            shift = (32 * h - 32 * i) % 128
            moved = far_parts[h] if shift == 0 else pltpu.roll(far_parts[h], shift, 1)
            packed = moved if packed is None else jnp.where(lane // 32 == h, moved, packed)
        pf_st[i] = packed
    start(*three("fp"))

    local(12, 16, {})

    arrived(*three("fp"))
    parts = [pf_st[0]] + [pf_r[i] for i in range(3)]
    far_m = parts[0][65:66]
    for part in parts[1:]:
        far_m = jnp.maximum(far_m, part[65:66])
    far = None
    for part in parts:
        scaled = part[:72] * jnp.exp2(part[65:66] - far_m)
        far = scaled if far is None else far + scaled
    row = lax.broadcasted_iota(jnp.int32, (72, 128), 0)
    far = jnp.where(row >= 65, far_m, far)
    src = lax.broadcasted_iota(jnp.int32, (128, 256), 0)
    dst = lax.broadcasted_iota(jnp.int32, (128, 256), 1)
    place = (src % 32) // 8 * 64 + 8 * zhi + src % 8 == dst
    active = (lax.broadcasted_iota(jnp.int32, (1, 256), 1) % 64) // 8 == zhi

    arrived("mp")
    half_lane = lax.broadcasted_iota(jnp.int32, (HEAD, 128), 1) < 64
    fixes = {}
    for h in range(HEADS):
        spread = jnp.dot(
            far, jnp.where(place & (src // 32 == h), 1.0, 0.0), precision=lax.Precision.HIGHEST, preferred_element_type=F32
        )
        n_f, d_f = spread[:HEAD], spread[HEAD:HEAD + 1]
        m_f = jnp.where(active, spread[65:66], NEG)
        n_a, d_a, m_a = pm_own[h, :HEAD], pm_own[h, HEAD:HEAD + 1], pm_own[h, HEAD + 1:HEAD + 2]
        n_b, d_b, m_b = pm_r[h, :HEAD], pm_r[h, HEAD:HEAD + 1], pm_r[h, HEAD + 1:HEAD + 2]
        top = jnp.maximum(jnp.maximum(m_a, m_b), m_f)
        w_a, w_b, w_f = jnp.exp2(m_a - top), jnp.exp2(m_b - top), jnp.exp2(m_f - top)
        num = w_a * n_a + w_b * n_b + w_f * n_f
        den = w_a * d_a + w_b * d_b + w_f * d_f
        for k in range(4):
            lanes = slice(k // 2 * 128, k // 2 * 128 + 128)
            n_m, d_m, m_m = num[:, lanes], den[:, lanes], top[:, lanes]
            if k % 2 != h % 2:
                n_m, d_m, m_m = (pltpu.roll(v, 64, 1) for v in (n_m, d_m, m_m))
            here = pl.ds(odd + 128 * (h // 2), 128)
            n_l = locacc[k, h, :HEAD, here]
            tail = locacc[k, h, HEAD:, here]
            d_l, m_l = tail[0:1], tail[1:2]
            peak = jnp.maximum(m_l, m_m)
            w_l, w_m = jnp.exp2(m_l - peak), jnp.exp2(m_m - peak)
            fixes[k, h] = (w_l * n_l + w_m * n_m) / (w_l * d_l + w_m * d_m)
    for k in range(4):
        for pair in range(2):
            both = jnp.where(half_lane, fixes[k, 2 * pair], fixes[k, 2 * pair + 1])
            fx_st[k, pair * HEAD:(pair + 1) * HEAD, :] = both.astype(BF16)
        if k < 3:
            start(f"f{k}")

    def contribution(k):
        att, fix = (att_st, fx_st) if k == 3 else (att_r, fx_r)
        side = pl.multiple_of(256 * ((core + RELATION[k]) % 2), 256)
        for h in range(HEADS):
            feats, here = pl.ds(h * HEAD, HEAD), pl.ds(side + 128 * (h // 2), 128)
            new = fix[k, h // 2 * HEAD:(h // 2 + 1) * HEAD, :]
            mine = half_lane if h % 2 == 0 else jnp.logical_not(half_lane)
            att[k, feats, here] = jnp.where(mine, new, att[k, feats, here])
        turned = att[k].astype(F32).T
        for m in range(64):
            for t in range(2):
                pp[t, pl.ds(8 * (m % 8) + m // 8, 8, stride=64), :] = turned[8 * m:8 * m + 8, 128 * t:128 * t + 128]
        rows = jnp.concatenate([pp[0], pp[1]], axis=1).astype(BF16)
        return dot(rows, wo[k]).astype(BF16).astype(F32)

    for n, k in enumerate((3, 2, 0, 1)):
        if k < 3:
            arrived(f"b{k}", f"f{k}")
        if k == 1:
            arrived("w2")
        if k == 2:
            arrived("wc")
        if n == 0:
            out_ref[...] = contribution(k)
        else:
            out_ref[...] += contribution(k)
    for name in COPIES:
        copy(name).wait_send()


def on_device(tokens, norm_gain, w_qkv, w_out):
    vm = pltpu.VMEM
    return pl.pallas_call(
        kernel,
        out_shape=jax.ShapeDtypeStruct((ROWS, 1024), F32),
        in_specs=[
            pl.BlockSpec(memory_space=pl.ANY),
            pl.BlockSpec(memory_space=pltpu.VMEM),
            pl.BlockSpec(memory_space=pl.ANY),
            pl.BlockSpec(memory_space=pl.ANY),
        ],
        out_specs=pl.BlockSpec(memory_space=pltpu.VMEM),
        scratch_shapes=[
            vm((4, ROWS, 1024), BF16),
            vm((3, 1024, FEATS), BF16),
            vm((ROWS, 1024), BF16),
            vm((6, ROWS, 128), F32),
            vm((HEADS, KEYS, 128), BF16),
            vm((HEADS, 128, KEYS), BF16),
            vm((HEADS, 80, KEYS), BF16),
            vm((4, HEADS, 256, 128), BF16),
            vm((2, 256, FEATS), BF16),
            vm((HEADS, 128, 512), BF16),
            vm((HEADS, 80, 1024), BF16),
            vm((HEADS, 32, 128), F32),
            vm((4, 4, HEADS, 32, 128), BF16),
            vm((32, FEATS), F32),
            vm((4, 32, FEATS), BF16),
            vm((HEADS, 128, 128), BF16),
            vm((HEADS, 80, 512), BF16),
            vm((HEADS, 72, 256), F32),
            vm((HEADS, 72, 256), F32),
            vm((HEADS, 72, 256), F32),
            vm((4, 72, 128), F32),
            vm((3, 72, 128), F32),
            vm((4, HEADS, 72, ROWS), F32),
            vm((4, FEATS, ROWS), BF16),
            vm((3, FEATS, ROWS), BF16),
            vm((4, 128, 128), BF16),
            vm((3, 128, 128), BF16),
            vm((4, FEATS, 1024), BF16),
            vm((KEYS, ROWS), F32),
            vm((KEYS, ROWS), F32),
            pltpu.SemaphoreType.DMA((len(COPIES),)),
            pltpu.SemaphoreType.DMA((len(COPIES),)),
            pltpu.SemaphoreType.DMA((4,)),
            pltpu.SemaphoreType.DMA((3,)),
            pltpu.SemaphoreType.DMA,
        ],
        compiler_params=pltpu.CompilerParams(
            collective_id=0, has_side_effects=True, vmem_limit_bytes=56 * 1024 * 1024
        ),
    )(tokens, norm_gain.reshape(1, 1024), jnp.transpose(w_qkv, (1, 0, 2)), w_out)


def solution(mesh):
    return jax.shard_map(
        on_device,
        mesh=mesh,
        in_specs=(P("seq", None), P(), P(None, None, "head"), P("head", None)),
        out_specs=P(("seq", "head"), None),
        check_vma=False,
    )
```

```python
import functools

import jax
import jax.numpy as jnp
from jax import lax
from jax.experimental import pallas as pl
from jax.experimental.pallas import tpu as pltpu
from jax.sharding import PartitionSpec as P

MESH = pl.DeviceIdType.MESH
F32 = jnp.float32
BF16 = jnp.bfloat16
EPS = 1e-05
LOG2E = 1.4426950408889634
HEADS = 4
HEAD = 64
ROWS = 512
FEATS = 256
KEYS = 2048
CHUNK = 256
NEG = -1e30

RELATION = (2, 3, 1, 0)

COPIES = (
    ["wc", "wz", "w2", "mq", "mp"]
    + [f"wy{i}" for i in (1, 2, 3)]
    + [f"wx{i}" for i in (1, 2, 3)]
    + [f"m{k}{i}" for k in range(4) for i in (1, 2, 3)]
    + [f"fz{i}" for i in (1, 2, 3)]
    + [f"fy{i}" for i in (1, 2, 3)]
    + [f"fq{i}" for i in (1, 2, 3)]
    + [f"fp{i}" for i in (1, 2, 3)]
    + [f"b{u}" for u in range(12)]
    + [f"f{i}" for i in range(3)]
)
SLOT = {name: i for i, name in enumerate(COPIES)}


def dot(a, b):
    return jnp.dot(a, b, preferred_element_type=F32)


def kernel(
    tokens_hbm, gain_ref, wqkv_hbm, wout_hbm, out_ref,
    tok, wq, normed, pp, kd, qt, vt, kvm, qm, qmp, vtm, kvff, kvf, qff, qf, qfp, vtf,
    pm_own, pm_st, pm_r, pf_st, pf_r, locacc, att_st, att_r, fx_st, fx_r, wo, s0, s1, s2, mid_all,
    send_sem, recv_sem, tok_sem, w_sem, wo_sem,
):
    seq = lax.axis_index("seq")
    g = lax.axis_index("head")
    zl, x, y = seq // 16, (seq // 4) % 4, seq % 4
    zhi, core = g // 2, g % 2

    def at_y(i):
        return (zl * 16 + x * 4 + (y + i) % 4, g)

    def at_x(i):
        return (zl * 16 + ((x + i) % 4) * 4 + y, g)

    def at_z(i):
        return (((zl + i) % 4) * 16 + x * 4 + y, g)

    x_pair = (zl * 16 + (x + 1 - 2 * (x % 2)) * 4 + y, g)

    def group(k):
        a, b = RELATION[k] // 2, RELATION[k] % 2
        return ((zhi + a) % 2) * 2 + (core + b) % 2

    def at_rel(k):
        return (seq, group(k))

    everyone = [at_y(i) for i in (1, 2, 3)] + [at_x(i) for i in (1, 2, 3)]
    everyone += [at_z(i) for i in (1, 2, 3)] + [at_rel(k) for k in (0, 1, 2)]
    barrier = pltpu.get_barrier_semaphore()
    for device in everyone:
        pl.semaphore_signal(barrier, inc=1, device_id=device, device_id_type=MESH)

    def unit_copy(u):
        k, feats = u // 4, pl.ds(pl.multiple_of(u % 4 * HEAD, HEAD), HEAD)
        there = ((zhi + 1 - k // 2) % 2) * 2 + (core + (k + 1) // 2) % 2
        return pltpu.make_async_remote_copy(
            src_ref=att_st.at[k, feats], dst_ref=att_r.at[k, feats],
            send_sem=send_sem.at[SLOT["b0"] + u], recv_sem=recv_sem.at[SLOT["b0"] + u],
            device_id=(seq, there), device_id_type=MESH,
        )

    def copy(name):
        piece = pl.ds(pl.multiple_of(16 * (x * 4 + y), 16), 16)
        quarter = pl.ds(pl.multiple_of(64 * x, 64), 64)
        kind, i = name[:-1], name[-1]
        if name == "wc":
            src, dst, dev = wo.at[3], wo.at[2], at_rel(2)
        elif name == "wz":
            src, dst, dev = wo.at[3, piece], wo.at[0, piece], at_rel(0)
        elif name == "w2":
            src, dst, dev = wo.at[0], wo.at[1], at_rel(2)
        elif name == "mq":
            src, dst, dev = qm.at[0], qm.at[1], x_pair
        elif name == "mp":
            src, dst, dev = pm_st, pm_r, x_pair
        elif kind == "wy":
            src, dst, dev = wo.at[0, piece], wo.at[0, piece], at_y(int(i))
        elif kind == "wx":
            src, dst, dev = wo.at[0, quarter], wo.at[0, quarter], at_x(int(i))
        elif kind[0] == "m":
            src, dst, dev = kvm.at[0, int(kind[1])], kvm.at[int(i), int(kind[1])], at_y(int(i))
        elif kind == "fz":
            src, dst, dev = kvf.at[0, 0], kvf.at[0, int(i)], at_z(int(i))
        elif kind == "fy":
            src, dst, dev = kvf.at[0], kvf.at[int(i)], at_y(int(i))
        elif kind == "fq":
            src, dst, dev = qf.at[0], qf.at[int(i)], at_x(int(i))
        elif kind == "fp":
            src, dst, dev = pf_st.at[int(i)], pf_r.at[int(i) - 1], at_x(4 - int(i))
        elif name[0] == "b":
            return unit_copy(int(name[1:]))
        else:
            src, dst, dev = fx_st.at[int(i)], fx_r.at[int(i)], at_rel(int(i))
        return pltpu.make_async_remote_copy(
            src_ref=src, dst_ref=dst, send_sem=send_sem.at[SLOT[name]], recv_sem=recv_sem.at[SLOT[name]],
            device_id=dev, device_id_type=MESH,
        )

    def start(*names):
        for name in names:
            copy(name).start()

    def arrived(*names):
        for name in names:
            copy(name).wait_recv()

    def three(kind):
        return [f"{kind}{i}" for i in (1, 2, 3)]

    def tok_copy(k):
        rows = pl.ds(pl.multiple_of(group(k) * ROWS, ROWS), ROWS)
        return pltpu.make_async_copy(tokens_hbm.at[rows], tok.at[k], tok_sem.at[k])

    w_copies = [pltpu.make_async_copy(wqkv_hbm.at[i], wq.at[i], w_sem.at[i]) for i in range(3)]
    wo_copy = pltpu.make_async_copy(wout_hbm, wo.at[3], wo_sem)
    tok_copy(0).start()
    for c in w_copies:
        c.start()
    wo_copy.start()
    for k in (1, 2, 3):
        tok_copy(k).start()

    vt[:, HEAD:, :] = jnp.ones((HEADS, 16, KEYS), BF16)
    vtm[:, HEAD:, :] = jnp.ones((HEADS, 16, 1024), BF16)
    vtf[:, HEAD:, :] = jnp.ones((HEADS, 16, 512), BF16)
    qmp[:, HEAD:, :] = jnp.zeros((HEADS, HEAD, 512), BF16)
    qfp[:, HEAD:, :] = jnp.zeros((HEADS, HEAD, 128), BF16)

    odd = pl.multiple_of(256 * core, 256)

    def norm_part(k, part):
        rows = pl.ds(part * 32, 32)
        wide = tok[k, rows, :].astype(F32)
        center = jnp.mean(wide, axis=1, keepdims=True)
        wide = wide - center
        variance = jnp.mean(wide * wide, axis=1, keepdims=True)
        normed[k % 2, rows, :] = (wide * lax.rsqrt(variance + EPS) * gain_ref[...]).astype(BF16)

    def project_part(k, i, half):
        result = dot(normed[k % 2, half * 256:(half + 1) * 256, :], wq[i])
        for m in range(32):
            b, c = half * 4 + m // 8, m % 8
            for t in range(2):
                pp[k % 2, 2 * i + t, pl.ds(8 * c + b, 8, stride=64), :] = result[8 * m:8 * m + 8, 128 * t:128 * t + 128]

    def piece(k, section, h, rows):
        return pp[k % 2, 2 * section + h // 2, rows, h % 2 * HEAD:h % 2 * HEAD + HEAD]

    def pick_part(k, h):
        feats = slice(h * HEAD, (h + 1) * HEAD)
        mid_rows = pl.ds(odd + h * 64, 64)
        far_rows = pl.ds(pl.multiple_of(odd + h * 64 + 8 * zhi, 8), 8)
        pair = jnp.concatenate([piece(k, 1, h, mid_rows), piece(k, 2, h, mid_rows)], axis=1)
        kvm[0, k, h] = pair.astype(BF16)
        qm[0, k * 64:(k + 1) * 64, feats] = piece(k, 0, h, mid_rows).astype(BF16)
        kvff[h, k * 8:(k + 1) * 8, :] = jnp.concatenate([piece(k, 1, h, far_rows), piece(k, 2, h, far_rows)], axis=1)
        qff[k * 8:(k + 1) * 8, feats] = piece(k, 0, h, far_rows)

    def key_part(k, h):
        key = piece(k, 1, h, slice(None))
        kd[h, pl.ds(k * ROWS, ROWS), :] = jnp.concatenate([key, key], axis=1).astype(BF16)

    def turn_part(k, pair):
        lanes = pl.ds(k * ROWS, ROWS)
        queries = pp[k % 2, pair].T.astype(BF16).astype(F32) * (0.125 * LOG2E)
        high = queries.astype(BF16)
        low = (queries - high.astype(F32)).astype(BF16)
        values = pp[k % 2, 4 + pair].T.astype(BF16)
        for side in range(2):
            feats = slice(side * HEAD, (side + 1) * HEAD)
            qt[2 * pair + side, :HEAD, lanes] = high[feats]
            qt[2 * pair + side, HEAD:, lanes] = low[feats]
            vt[2 * pair + side, :HEAD, lanes] = values[feats]

    tok_copy(0).wait()
    for part in range(16):
        norm_part(0, part)
    for c in w_copies:
        c.wait()
    for k in range(5):
        mxu = [functools.partial(project_part, k, i, side) for i in (1, 2, 0) for side in range(2)] if k < 4 else []
        beside = []
        if k > 0:
            beside += [functools.partial(pick_part, k - 1, h) for h in range(HEADS)]
        if k < 3:
            tok_copy(k + 1).wait()
            beside += [functools.partial(norm_part, k + 1, part) for part in range(16)]
        if k > 0:
            beside += [functools.partial(key_part, k - 1, h) for h in range(HEADS)]
            beside += [functools.partial(turn_part, k - 1, pair) for pair in range(2)]
        for n in range(max(len(mxu), 1)):
            if mxu:
                mxu[n]()
            share = len(beside) / max(len(mxu), 1)
            for item in beside[round(n * share):round((n + 1) * share)]:
                item()
        if k == 0:
            pl.semaphore_wait(barrier, len(everyone))
            wo_copy.wait()
            start("wc", "wz")
        else:
            start(*three(f"m{k - 1}"))
        if k == 3:
            arrived("wz")
            start(*three("wy"))
    kvf[0, 0] = kvff[...].astype(BF16)
    qf[0] = qff[...].astype(BF16)
    start(*three("fz"), "mq", *three("fq"))

    def top_rows(den8, m):
        row = lax.broadcasted_iota(jnp.int32, den8.shape, 0)
        return jnp.where(row == 0, den8, m)

    def scores(u, slot, c, peak):
        k, h = u // 4, u % 4
        lanes = pl.ds(pl.multiple_of(k * ROWS, ROWS), ROWS)
        s = dot(kd[h, c * CHUNK:(c + 1) * CHUNK, :], qt[h, :, lanes])
        slot[c * CHUNK:(c + 1) * CHUNK, :] = s
        t = jnp.max(s.reshape(CHUNK // 8, 8, ROWS), axis=0)
        return t if peak is None else jnp.maximum(peak, t)

    def weigh(u, slot, c, m, acc):
        h = u % 4
        p = jnp.exp2(slot[c * CHUNK:(c + 1) * CHUNK, :] - m).astype(BF16)
        o = dot(vt[h, :, c * CHUNK:(c + 1) * CHUNK], p)
        return o if acc is None else acc + o

    def finish(u, acc, m):
        k, h = u // 4, u % 4
        feats = pl.ds(pl.multiple_of(h * HEAD, HEAD), HEAD)
        att_st[k, feats, :] = (acc[:HEAD] * (1.0 / acc[HEAD:HEAD + 1])).astype(BF16)
        locacc[k, h, :HEAD, :] = acc[:HEAD]
        locacc[k, h, HEAD:, :] = top_rows(acc[HEAD:HEAD + 8], m)

    def half(u, cur, nxt, m, last=False):
        peak = acc = None
        for c in range(KEYS // CHUNK):
            if not last:
                peak = scores(u + 1, nxt, c, peak)
            acc = weigh(u, cur, c, m, acc)
        finish(u, acc, m)
        return None if last else jnp.max(peak, axis=0, keepdims=True)

    def local(first, m):
        def body(i, m):
            u = first + 2 * i
            m = half(u, s0, s1, m)
            if first < 12:
                unit_copy(u).start()
            m = half(u + 1, s1, s0, m)
            if first < 12:
                unit_copy(u + 1).start()
            return m

        return lax.fori_loop(0, 2, body, m)

    peak = None
    for c in range(KEYS // CHUNK):
        peak = scores(0, s0, c, peak)
    local_m = local(0, jnp.max(peak, axis=0, keepdims=True))
    arrived(*three("fz"), *three("wy"))
    start(*three("fy"), *three("wx"))

    arrived("mq", *[name for k in range(4) for name in three(f"m{k}")])
    for i in range(2):
        turned = (qm[i].astype(F32) * 0.125).T.astype(BF16)
        for h in range(HEADS):
            qmp[h, :HEAD, i * 256:(i + 1) * 256] = turned[h * HEAD:(h + 1) * HEAD]
    for i in range(4):
        for h in range(HEADS):
            vtm[h, :HEAD, i * 256:(i + 1) * 256] = kvm[i, :, h].reshape(256, 128).astype(F32).T[HEAD:].astype(BF16)

    def mid_scores(h, slot, c, peak):
        s = dot(kvm[c, :, h].reshape(256, 128), qmp[h]) * LOG2E
        slot[c * CHUNK:(c + 1) * CHUNK, :] = s
        t = jnp.max(s.reshape(CHUNK // 8, 8, 512), axis=0)
        return t if peak is None else jnp.maximum(peak, t)

    def mid_weigh(h, slot, c, m, acc):
        p = jnp.exp2(slot[c * CHUNK:(c + 1) * CHUNK, :] - m).astype(BF16)
        o = dot(vtm[h, :, c * CHUNK:(c + 1) * CHUNK], p)
        return o if acc is None else acc + o

    peak = None
    for c in range(4):
        peak = mid_scores(0, s1, c, peak)
    for h in range(HEADS):
        cur, nxt = (s1, s2) if h % 2 == 0 else (s2, s1)
        m = jnp.max(peak, axis=0, keepdims=True)
        peak = acc = None
        for c in range(4):
            if h < 3:
                peak = mid_scores(h + 1, nxt, c, peak)
            acc = mid_weigh(h, cur, c, m, acc)
        tail = top_rows(acc[HEAD:HEAD + 8], m)
        pm_st[h, :HEAD, :] = acc[:HEAD, 256:]
        pm_st[h, HEAD:, :] = tail[:, 256:]
        pm_own[h, :HEAD, :] = acc[:HEAD, :256]
        pm_own[h, HEAD:, :] = tail[:, :256]
    start("mp")

    local_m = local(4, local_m)
    arrived(*three("wx"))
    start("w2")

    arrived(*three("fy"), *three("fq"))
    gathered = jnp.concatenate([qf[i] for i in range(4)], axis=0)
    turned = (gathered.astype(F32) * 0.125).T.astype(BF16)
    far_parts = []
    for h in range(HEADS):
        qfp[h, :HEAD, :] = turned[h * HEAD:(h + 1) * HEAD]
        keyval = kvf[:, :, h].reshape(512, 128)
        vtf[h, :HEAD, :] = keyval.astype(F32).T[HEAD:].astype(BF16)
        s = dot(keyval, qfp[h]) * LOG2E
        m = jnp.max(s, axis=0, keepdims=True)
        p = jnp.exp2(s - m).astype(BF16)
        acc = dot(vtf[h], p)
        far_parts.append(jnp.concatenate([acc[:HEAD], top_rows(acc[HEAD:HEAD + 8], m)], axis=0))
    lane = lax.broadcasted_iota(jnp.int32, (72, 128), 1)
    for i in range(4):
        packed = None
        for h in range(HEADS):
            shift = (32 * h - 32 * i) % 128
            moved = far_parts[h] if shift == 0 else pltpu.roll(far_parts[h], shift, 1)
            packed = moved if packed is None else jnp.where(lane // 32 == h, moved, packed)
        pf_st[i] = packed
    start(*three("fp"))

    local_m = local(8, local_m)

    arrived(*three("fp"))
    parts = [pf_st[0]] + [pf_r[i] for i in range(3)]
    far_m = parts[0][65:66]
    for part in parts[1:]:
        far_m = jnp.maximum(far_m, part[65:66])
    far = None
    for part in parts:
        scaled = part[:72] * jnp.exp2(part[65:66] - far_m)
        far = scaled if far is None else far + scaled
    row = lax.broadcasted_iota(jnp.int32, (72, 128), 0)
    far = jnp.where(row >= 65, far_m, far)
    src = lax.broadcasted_iota(jnp.int32, (128, 256), 0)
    dst = lax.broadcasted_iota(jnp.int32, (128, 256), 1)
    place = (src % 32) // 8 * 64 + 8 * zhi + src % 8 == dst
    active = (lax.broadcasted_iota(jnp.int32, (1, 256), 1) % 64) // 8 == zhi

    arrived("mp")
    half_lane = lax.broadcasted_iota(jnp.int32, (HEAD, 128), 1) < 64
    for h in range(HEADS):
        spread = jnp.dot(
            far, jnp.where(place & (src // 32 == h), 1.0, 0.0), precision=lax.Precision.HIGHEST, preferred_element_type=F32
        )
        n_f, d_f = spread[:HEAD], spread[HEAD:HEAD + 1]
        m_f = jnp.where(active, spread[65:66], NEG)
        n_a, d_a, m_a = pm_own[h, :HEAD], pm_own[h, HEAD:HEAD + 1], pm_own[h, HEAD + 1:HEAD + 2]
        n_b, d_b, m_b = pm_r[h, :HEAD], pm_r[h, HEAD:HEAD + 1], pm_r[h, HEAD + 1:HEAD + 2]
        top = jnp.maximum(jnp.maximum(m_a, m_b), m_f)
        w_a, w_b, w_f = jnp.exp2(m_a - top), jnp.exp2(m_b - top), jnp.exp2(m_f - top)
        num = w_a * n_a + w_b * n_b + w_f * n_f
        den = w_a * d_a + w_b * d_b + w_f * d_f
        mid_all[h, :HEAD, :] = num
        mid_all[h, HEAD:, :] = top_rows(jnp.broadcast_to(den, (8, 256)), top)

    def fix_block(k):
        lanes = slice(k // 2 * 128, k // 2 * 128 + 128)
        fixed = []
        for h in range(HEADS):
            n_m, tail = mid_all[h, :HEAD, lanes], mid_all[h, HEAD:, lanes]
            if k % 2 != h % 2:
                n_m, tail = pltpu.roll(n_m, 64, 1), pltpu.roll(tail, 64, 1)
            d_m, m_m = tail[0:1], tail[1:2]
            here = pl.ds(odd + 128 * (h // 2), 128)
            n_l = locacc[k, h, :HEAD, here]
            tail = locacc[k, h, HEAD:, here]
            d_l, m_l = tail[0:1], tail[1:2]
            peak = jnp.maximum(m_l, m_m)
            w_l, w_m = jnp.exp2(m_l - peak), jnp.exp2(m_m - peak)
            fixed.append((w_l * n_l + w_m * n_m) / (w_l * d_l + w_m * d_m))
        for pair in range(2):
            both = jnp.where(half_lane, fixed[2 * pair], fixed[2 * pair + 1])
            fx_st[k, pair * HEAD:(pair + 1) * HEAD, :] = both.astype(BF16)

    for k in range(3):
        fix_block(k)
        start(f"f{k}")

    local_m = half(12, s0, s1, local_m)
    local_m = half(13, s1, s0, local_m)
    local_m = half(14, s0, s1, local_m)
    half(15, s1, s0, local_m, last=True)
    fix_block(3)

    def contribution(k):
        att, fix = (att_st, fx_st) if k == 3 else (att_r, fx_r)
        side = pl.multiple_of(256 * ((core + RELATION[k]) % 2), 256)
        for h in range(HEADS):
            feats, here = pl.ds(h * HEAD, HEAD), pl.ds(side + 128 * (h // 2), 128)
            new = fix[k, h // 2 * HEAD:(h // 2 + 1) * HEAD, :]
            mine = half_lane if h % 2 == 0 else jnp.logical_not(half_lane)
            att[k, feats, here] = jnp.where(mine, new, att[k, feats, here])
        turned = att[k].astype(F32).T
        for m in range(64):
            for t in range(2):
                pp[0, t, pl.ds(8 * (m % 8) + m // 8, 8, stride=64), :] = turned[8 * m:8 * m + 8, 128 * t:128 * t + 128]
        rows = jnp.concatenate([pp[0, 0], pp[0, 1]], axis=1).astype(BF16)
        return dot(rows, wo[k]).astype(BF16).astype(F32)

    for n, k in enumerate((3, 2, 0, 1)):
        if k < 3:
            arrived(*[f"b{4 * k + h}" for h in range(HEADS)], f"f{k}")
        if k == 1:
            arrived("w2")
        if k == 2:
            arrived("wc")
        if n == 0:
            out_ref[...] = contribution(k)
        else:
            out_ref[...] += contribution(k)
    for name in COPIES:
        copy(name).wait_send()


def on_device(tokens, norm_gain, w_qkv, w_out):
    vm = pltpu.VMEM
    return pl.pallas_call(
        kernel,
        out_shape=jax.ShapeDtypeStruct((ROWS, 1024), F32),
        in_specs=[
            pl.BlockSpec(memory_space=pl.ANY),
            pl.BlockSpec(memory_space=pltpu.VMEM),
            pl.BlockSpec(memory_space=pl.ANY),
            pl.BlockSpec(memory_space=pl.ANY),
        ],
        out_specs=pl.BlockSpec(memory_space=pltpu.VMEM),
        scratch_shapes=[
            vm((4, ROWS, 1024), BF16),
            vm((3, 1024, FEATS), BF16),
            vm((2, ROWS, 1024), BF16),
            vm((2, 6, ROWS, 128), F32),
            vm((HEADS, KEYS, 128), BF16),
            vm((HEADS, 128, KEYS), BF16),
            vm((HEADS, 80, KEYS), BF16),
            vm((4, 4, HEADS, 64, 128), BF16),
            vm((2, 256, FEATS), BF16),
            vm((HEADS, 128, 512), BF16),
            vm((HEADS, 80, 1024), BF16),
            vm((HEADS, 32, 128), F32),
            vm((4, 4, HEADS, 32, 128), BF16),
            vm((32, FEATS), F32),
            vm((4, 32, FEATS), BF16),
            vm((HEADS, 128, 128), BF16),
            vm((HEADS, 80, 512), BF16),
            vm((HEADS, 72, 256), F32),
            vm((HEADS, 72, 256), F32),
            vm((HEADS, 72, 256), F32),
            vm((4, 72, 128), F32),
            vm((3, 72, 128), F32),
            vm((4, HEADS, 72, ROWS), F32),
            vm((4, FEATS, ROWS), BF16),
            vm((3, FEATS, ROWS), BF16),
            vm((4, 128, 128), BF16),
            vm((3, 128, 128), BF16),
            vm((4, FEATS, 1024), BF16),
            vm((KEYS, ROWS), F32),
            vm((KEYS, ROWS), F32),
            vm((1024, ROWS), F32),
            vm((HEADS, 72, 256), F32),
            pltpu.SemaphoreType.DMA((len(COPIES),)),
            pltpu.SemaphoreType.DMA((len(COPIES),)),
            pltpu.SemaphoreType.DMA((4,)),
            pltpu.SemaphoreType.DMA((3,)),
            pltpu.SemaphoreType.DMA,
        ],
        compiler_params=pltpu.CompilerParams(
            collective_id=0, has_side_effects=True, vmem_limit_bytes=56 * 1024 * 1024
        ),
    )(tokens, norm_gain.reshape(1, 1024), jnp.transpose(w_qkv, (1, 0, 2)), w_out)


def solution(mesh):
    return jax.shard_map(
        on_device,
        mesh=mesh,
        in_specs=(P("seq", None), P(), P(None, None, "head"), P("head", None)),
        out_specs=P(("seq", "head"), None),
        check_vma=False,
    )
```

```python
import functools

import jax
import jax.numpy as jnp
from jax import lax
from jax.experimental import pallas as pl
from jax.experimental.pallas import tpu as pltpu
from jax.sharding import PartitionSpec as P

MESH = pl.DeviceIdType.MESH
F32 = jnp.float32
BF16 = jnp.bfloat16
EPS = 1e-05
LOG2E = 1.4426950408889634
HEADS = 4
HEAD = 64
ROWS = 512
FEATS = 256
KEYS = 2048
CHUNK = 256
NEG = -1e30

RELATION = (2, 3, 1, 0)

COPIES = (
    ["wc", "wz", "w2", "mq", "mp"]
    + [f"wy{i}" for i in (1, 2, 3)]
    + [f"wx{i}" for i in (1, 2, 3)]
    + [f"m{k}{i}" for k in range(4) for i in (1, 2, 3)]
    + [f"fz{i}" for i in (1, 2, 3)]
    + [f"fy{i}" for i in (1, 2, 3)]
    + [f"fq{i}" for i in (1, 2, 3)]
    + [f"fp{i}" for i in (1, 2, 3)]
    + [f"b{u}" for u in range(12)]
    + [f"f{i}" for i in range(3)]
)
SLOT = {name: i for i, name in enumerate(COPIES)}


def dot(a, b):
    return jnp.dot(a, b, preferred_element_type=F32)


def kernel(
    tokens_hbm, gain_ref, wqkv_hbm, wout_hbm, out_ref,
    tok, wq, normed, pp, kd, qt, vt, kvm, qm, qmp, vtm, kvff, kvf, qff, qf, qfp, vtf,
    pm_own, pm_st, pm_r, pf_st, pf_r, locacc, att_st, att_r, fx_st, fx_r, wo, s0, s1, s2, mid_all,
    send_sem, recv_sem, tok_sem, w_sem, wo_sem, total, out_sem,
):
    seq = lax.axis_index("seq")
    g = lax.axis_index("head")
    zl, x, y = seq // 16, (seq // 4) % 4, seq % 4
    zhi, core = g // 2, g % 2

    def at_y(i):
        return (zl * 16 + x * 4 + (y + i) % 4, g)

    def at_x(i):
        return (zl * 16 + ((x + i) % 4) * 4 + y, g)

    def at_z(i):
        return (((zl + i) % 4) * 16 + x * 4 + y, g)

    x_pair = (zl * 16 + (x + 1 - 2 * (x % 2)) * 4 + y, g)

    def group(k):
        a, b = RELATION[k] // 2, RELATION[k] % 2
        return ((zhi + a) % 2) * 2 + (core + b) % 2

    def at_rel(k):
        return (seq, group(k))

    everyone = [at_y(i) for i in (1, 2, 3)] + [at_x(i) for i in (1, 2, 3)]
    everyone += [at_z(i) for i in (1, 2, 3)] + [at_rel(k) for k in (0, 1, 2)]
    barrier = pltpu.get_barrier_semaphore()
    for device in everyone:
        pl.semaphore_signal(barrier, inc=1, device_id=device, device_id_type=MESH)

    def unit_copy(u):
        k, feats = u // 4, pl.ds(pl.multiple_of(u % 4 * HEAD, HEAD), HEAD)
        there = ((zhi + 1 - k // 2) % 2) * 2 + (core + (k + 1) // 2) % 2
        return pltpu.make_async_remote_copy(
            src_ref=att_st.at[k, feats], dst_ref=att_r.at[k, feats],
            send_sem=send_sem.at[SLOT["b0"] + u], recv_sem=recv_sem.at[SLOT["b0"] + u],
            device_id=(seq, there), device_id_type=MESH,
        )

    def copy(name):
        piece = pl.ds(pl.multiple_of(16 * (x * 4 + y), 16), 16)
        quarter = pl.ds(pl.multiple_of(64 * x, 64), 64)
        kind, i = name[:-1], name[-1]
        if name == "wc":
            src, dst, dev = wo.at[3], wo.at[2], at_rel(2)
        elif name == "wz":
            src, dst, dev = wo.at[3, piece], wo.at[0, piece], at_rel(0)
        elif name == "w2":
            src, dst, dev = wo.at[0], wo.at[1], at_rel(2)
        elif name == "mq":
            src, dst, dev = qm.at[0], qm.at[1], x_pair
        elif name == "mp":
            src, dst, dev = pm_st, pm_r, x_pair
        elif kind == "wy":
            src, dst, dev = wo.at[0, piece], wo.at[0, piece], at_y(int(i))
        elif kind == "wx":
            src, dst, dev = wo.at[0, quarter], wo.at[0, quarter], at_x(int(i))
        elif kind[0] == "m":
            src, dst, dev = kvm.at[0, int(kind[1])], kvm.at[int(i), int(kind[1])], at_y(int(i))
        elif kind == "fz":
            src, dst, dev = kvf.at[0, 0], kvf.at[0, int(i)], at_z(int(i))
        elif kind == "fy":
            src, dst, dev = kvf.at[0], kvf.at[int(i)], at_y(int(i))
        elif kind == "fq":
            src, dst, dev = qf.at[0], qf.at[int(i)], at_x(int(i))
        elif kind == "fp":
            src, dst, dev = pf_st.at[int(i)], pf_r.at[int(i) - 1], at_x(4 - int(i))
        elif name[0] == "b":
            return unit_copy(int(name[1:]))
        else:
            src, dst, dev = fx_st.at[int(i)], fx_r.at[int(i)], at_rel(int(i))
        return pltpu.make_async_remote_copy(
            src_ref=src, dst_ref=dst, send_sem=send_sem.at[SLOT[name]], recv_sem=recv_sem.at[SLOT[name]],
            device_id=dev, device_id_type=MESH,
        )

    def start(*names):
        for name in names:
            copy(name).start()

    def arrived(*names):
        for name in names:
            copy(name).wait_recv()

    def three(kind):
        return [f"{kind}{i}" for i in (1, 2, 3)]

    def tok_copy(k):
        rows = pl.ds(pl.multiple_of(group(k) * ROWS, ROWS), ROWS)
        return pltpu.make_async_copy(tokens_hbm.at[rows], tok.at[k], tok_sem.at[k])

    w_copies = [pltpu.make_async_copy(wqkv_hbm.at[i], wq.at[i], w_sem.at[i]) for i in range(3)]
    wo_copy = pltpu.make_async_copy(wout_hbm, wo.at[3], wo_sem)
    tok_copy(0).start()
    for c in w_copies:
        c.start()
    wo_copy.start()
    for k in (1, 2, 3):
        tok_copy(k).start()

    vt[:, HEAD:, :] = jnp.ones((HEADS, 16, KEYS), BF16)
    vtm[:, HEAD:, :] = jnp.ones((HEADS, 16, 1024), BF16)
    vtf[:, HEAD:, :] = jnp.ones((HEADS, 16, 512), BF16)
    qmp[:, HEAD:, :] = jnp.zeros((HEADS, HEAD, 512), BF16)
    qfp[:, HEAD:, :] = jnp.zeros((HEADS, HEAD, 128), BF16)

    odd = pl.multiple_of(256 * core, 256)

    def norm_part(k, part):
        rows = pl.ds(part * 32, 32)
        wide = tok[k, rows, :].astype(F32)
        center = jnp.mean(wide, axis=1, keepdims=True)
        wide = wide - center
        variance = jnp.mean(wide * wide, axis=1, keepdims=True)
        normed[k % 2, rows, :] = (wide * lax.rsqrt(variance + EPS) * gain_ref[...]).astype(BF16)

    def project_part(k, i, half):
        result = dot(normed[k % 2, half * 256:(half + 1) * 256, :], wq[i])
        for m in range(32):
            b, c = half * 4 + m // 8, m % 8
            for t in range(2):
                pp[k % 2, 2 * i + t, pl.ds(8 * c + b, 8, stride=64), :] = result[8 * m:8 * m + 8, 128 * t:128 * t + 128]

    def piece(k, section, h, rows):
        return pp[k % 2, 2 * section + h // 2, rows, h % 2 * HEAD:h % 2 * HEAD + HEAD]

    def pick_part(k, h):
        feats = slice(h * HEAD, (h + 1) * HEAD)
        mid_rows = pl.ds(odd + h * 64, 64)
        far_rows = pl.ds(pl.multiple_of(odd + h * 64 + 8 * zhi, 8), 8)
        pair = jnp.concatenate([piece(k, 1, h, mid_rows), piece(k, 2, h, mid_rows)], axis=1)
        kvm[0, k, h] = pair.astype(BF16)
        qm[0, k * 64:(k + 1) * 64, feats] = piece(k, 0, h, mid_rows).astype(BF16)
        kvff[h, k * 8:(k + 1) * 8, :] = jnp.concatenate([piece(k, 1, h, far_rows), piece(k, 2, h, far_rows)], axis=1)
        qff[k * 8:(k + 1) * 8, feats] = piece(k, 0, h, far_rows)

    def key_part(k, h):
        key = piece(k, 1, h, slice(None))
        kd[h, pl.ds(k * ROWS, ROWS), :] = jnp.concatenate([key, key], axis=1).astype(BF16)

    def turn_part(k, pair):
        lanes = pl.ds(k * ROWS, ROWS)
        queries = pp[k % 2, pair].T.astype(BF16).astype(F32) * (0.125 * LOG2E)
        high = queries.astype(BF16)
        low = (queries - high.astype(F32)).astype(BF16)
        values = pp[k % 2, 4 + pair].T.astype(BF16)
        for side in range(2):
            feats = slice(side * HEAD, (side + 1) * HEAD)
            qt[2 * pair + side, :HEAD, lanes] = high[feats]
            qt[2 * pair + side, HEAD:, lanes] = low[feats]
            vt[2 * pair + side, :HEAD, lanes] = values[feats]

    tok_copy(0).wait()
    for part in range(16):
        norm_part(0, part)
    for c in w_copies:
        c.wait()
    for k in range(5):
        mxu = [functools.partial(project_part, k, i, side) for i in (1, 2, 0) for side in range(2)] if k < 4 else []
        beside = []
        if k > 0:
            beside += [functools.partial(pick_part, k - 1, h) for h in range(HEADS)]
        if k < 3:
            tok_copy(k + 1).wait()
            beside += [functools.partial(norm_part, k + 1, part) for part in range(16)]
        if k > 0:
            beside += [functools.partial(key_part, k - 1, h) for h in range(HEADS)]
            beside += [functools.partial(turn_part, k - 1, pair) for pair in range(2)]
        for n in range(max(len(mxu), 1)):
            if mxu:
                mxu[n]()
            share = len(beside) / max(len(mxu), 1)
            for item in beside[round(n * share):round((n + 1) * share)]:
                item()
        if k == 0:
            pl.semaphore_wait(barrier, len(everyone))
            wo_copy.wait()
            start("wc", "wz")
        else:
            start(*three(f"m{k - 1}"))
        if k == 3:
            arrived("wz")
            start(*three("wy"))
    kvf[0, 0] = kvff[...].astype(BF16)
    qf[0] = qff[...].astype(BF16)
    start(*three("fz"), "mq", *three("fq"))

    def top_rows(den8, m):
        row = lax.broadcasted_iota(jnp.int32, den8.shape, 0)
        return jnp.where(row == 0, den8, m)

    def scores(u, slot, c, peak):
        k, h = u // 4, u % 4
        lanes = pl.ds(pl.multiple_of(k * ROWS, ROWS), ROWS)
        s = dot(kd[h, c * CHUNK:(c + 1) * CHUNK, :], qt[h, :, lanes])
        slot[c * CHUNK:(c + 1) * CHUNK, :] = s
        t = jnp.max(s.reshape(CHUNK // 8, 8, ROWS), axis=0)
        return t if peak is None else jnp.maximum(peak, t)

    def weigh(u, slot, c, m, acc):
        h = u % 4
        p = jnp.exp2(slot[c * CHUNK:(c + 1) * CHUNK, :] - m).astype(BF16)
        o = dot(vt[h, :, c * CHUNK:(c + 1) * CHUNK], p)
        return o if acc is None else acc + o

    def finish(u, acc, m):
        k, h = u // 4, u % 4
        feats = pl.ds(pl.multiple_of(h * HEAD, HEAD), HEAD)
        att_st[k, feats, :] = (acc[:HEAD] * (1.0 / acc[HEAD:HEAD + 1])).astype(BF16)
        locacc[k, h, :HEAD, :] = acc[:HEAD]
        locacc[k, h, HEAD:, :] = top_rows(acc[HEAD:HEAD + 8], m)

    def half(u, cur, nxt, m, last=False):
        peak = acc = None
        for c in range(KEYS // CHUNK):
            if not last:
                peak = scores(u + 1, nxt, c, peak)
            acc = weigh(u, cur, c, m, acc)
        finish(u, acc, m)
        return None if last else jnp.max(peak, axis=0, keepdims=True)

    def local(first, m):
        def body(i, m):
            u = first + 2 * i
            m = half(u, s0, s1, m)
            if first < 12:
                unit_copy(u).start()
            m = half(u + 1, s1, s0, m)
            if first < 12:
                unit_copy(u + 1).start()
            return m

        return lax.fori_loop(0, 2, body, m)

    peak = None
    for c in range(KEYS // CHUNK):
        peak = scores(0, s0, c, peak)
    local_m = local(0, jnp.max(peak, axis=0, keepdims=True))
    arrived(*three("fz"), *three("wy"))
    start(*three("fy"), *three("wx"))

    arrived("mq", *[name for k in range(4) for name in three(f"m{k}")])
    for i in range(2):
        turned = (qm[i].astype(F32) * 0.125).T.astype(BF16)
        for h in range(HEADS):
            qmp[h, :HEAD, i * 256:(i + 1) * 256] = turned[h * HEAD:(h + 1) * HEAD]
    for i in range(4):
        for h in range(HEADS):
            vtm[h, :HEAD, i * 256:(i + 1) * 256] = kvm[i, :, h].reshape(256, 128).astype(F32).T[HEAD:].astype(BF16)

    def mid_scores(h, slot, c, peak):
        s = dot(kvm[c, :, h].reshape(256, 128), qmp[h]) * LOG2E
        slot[c * CHUNK:(c + 1) * CHUNK, :] = s
        t = jnp.max(s.reshape(CHUNK // 8, 8, 512), axis=0)
        return t if peak is None else jnp.maximum(peak, t)

    def mid_weigh(h, slot, c, m, acc):
        p = jnp.exp2(slot[c * CHUNK:(c + 1) * CHUNK, :] - m).astype(BF16)
        o = dot(vtm[h, :, c * CHUNK:(c + 1) * CHUNK], p)
        return o if acc is None else acc + o

    peak = None
    for c in range(4):
        peak = mid_scores(0, s1, c, peak)
    for h in range(HEADS):
        cur, nxt = (s1, s2) if h % 2 == 0 else (s2, s1)
        m = jnp.max(peak, axis=0, keepdims=True)
        peak = acc = None
        for c in range(4):
            if h < 3:
                peak = mid_scores(h + 1, nxt, c, peak)
            acc = mid_weigh(h, cur, c, m, acc)
        tail = top_rows(acc[HEAD:HEAD + 8], m)
        pm_st[h, :HEAD, :] = acc[:HEAD, 256:]
        pm_st[h, HEAD:, :] = tail[:, 256:]
        pm_own[h, :HEAD, :] = acc[:HEAD, :256]
        pm_own[h, HEAD:, :] = tail[:, :256]
    start("mp")

    local_m = local(4, local_m)
    arrived(*three("wx"))
    start("w2")

    arrived(*three("fy"), *three("fq"))
    gathered = jnp.concatenate([qf[i] for i in range(4)], axis=0)
    turned = (gathered.astype(F32) * 0.125).T.astype(BF16)
    far_parts = []
    for h in range(HEADS):
        qfp[h, :HEAD, :] = turned[h * HEAD:(h + 1) * HEAD]
        keyval = kvf[:, :, h].reshape(512, 128)
        vtf[h, :HEAD, :] = keyval.astype(F32).T[HEAD:].astype(BF16)
        s = dot(keyval, qfp[h]) * LOG2E
        m = jnp.max(s, axis=0, keepdims=True)
        p = jnp.exp2(s - m).astype(BF16)
        acc = dot(vtf[h], p)
        far_parts.append(jnp.concatenate([acc[:HEAD], top_rows(acc[HEAD:HEAD + 8], m)], axis=0))
    lane = lax.broadcasted_iota(jnp.int32, (72, 128), 1)
    for i in range(4):
        packed = None
        for h in range(HEADS):
            shift = (32 * h - 32 * i) % 128
            moved = far_parts[h] if shift == 0 else pltpu.roll(far_parts[h], shift, 1)
            packed = moved if packed is None else jnp.where(lane // 32 == h, moved, packed)
        pf_st[i] = packed
    start(*three("fp"))

    local_m = local(8, local_m)

    arrived(*three("fp"))
    parts = [pf_st[0]] + [pf_r[i] for i in range(3)]
    far_m = parts[0][65:66]
    for part in parts[1:]:
        far_m = jnp.maximum(far_m, part[65:66])
    far = None
    for part in parts:
        scaled = part[:72] * jnp.exp2(part[65:66] - far_m)
        far = scaled if far is None else far + scaled
    row = lax.broadcasted_iota(jnp.int32, (72, 128), 0)
    far = jnp.where(row >= 65, far_m, far)
    src = lax.broadcasted_iota(jnp.int32, (128, 256), 0)
    dst = lax.broadcasted_iota(jnp.int32, (128, 256), 1)
    place = (src % 32) // 8 * 64 + 8 * zhi + src % 8 == dst
    active = (lax.broadcasted_iota(jnp.int32, (1, 256), 1) % 64) // 8 == zhi

    arrived("mp")
    half_lane = lax.broadcasted_iota(jnp.int32, (HEAD, 128), 1) < 64
    for h in range(HEADS):
        spread = jnp.dot(
            far, jnp.where(place & (src // 32 == h), 1.0, 0.0), precision=lax.Precision.HIGHEST, preferred_element_type=F32
        )
        n_f, d_f = spread[:HEAD], spread[HEAD:HEAD + 1]
        m_f = jnp.where(active, spread[65:66], NEG)
        n_a, d_a, m_a = pm_own[h, :HEAD], pm_own[h, HEAD:HEAD + 1], pm_own[h, HEAD + 1:HEAD + 2]
        n_b, d_b, m_b = pm_r[h, :HEAD], pm_r[h, HEAD:HEAD + 1], pm_r[h, HEAD + 1:HEAD + 2]
        top = jnp.maximum(jnp.maximum(m_a, m_b), m_f)
        w_a, w_b, w_f = jnp.exp2(m_a - top), jnp.exp2(m_b - top), jnp.exp2(m_f - top)
        num = w_a * n_a + w_b * n_b + w_f * n_f
        den = w_a * d_a + w_b * d_b + w_f * d_f
        mid_all[h, :HEAD, :] = num
        mid_all[h, HEAD:, :] = top_rows(jnp.broadcast_to(den, (8, 256)), top)

    def fix_block(k):
        lanes = slice(k // 2 * 128, k // 2 * 128 + 128)
        fixed = []
        for h in range(HEADS):
            n_m, tail = mid_all[h, :HEAD, lanes], mid_all[h, HEAD:, lanes]
            if k % 2 != h % 2:
                n_m, tail = pltpu.roll(n_m, 64, 1), pltpu.roll(tail, 64, 1)
            d_m, m_m = tail[0:1], tail[1:2]
            here = pl.ds(odd + 128 * (h // 2), 128)
            n_l = locacc[k, h, :HEAD, here]
            tail = locacc[k, h, HEAD:, here]
            d_l, m_l = tail[0:1], tail[1:2]
            peak = jnp.maximum(m_l, m_m)
            w_l, w_m = jnp.exp2(m_l - peak), jnp.exp2(m_m - peak)
            fixed.append((w_l * n_l + w_m * n_m) / (w_l * d_l + w_m * d_m))
        for pair in range(2):
            both = jnp.where(half_lane, fixed[2 * pair], fixed[2 * pair + 1])
            fx_st[k, pair * HEAD:(pair + 1) * HEAD, :] = both.astype(BF16)

    for k in range(3):
        fix_block(k)
        start(f"f{k}")

    local_m = half(12, s0, s1, local_m)
    local_m = half(13, s1, s0, local_m)
    local_m = half(14, s0, s1, local_m)
    half(15, s1, s0, local_m, last=True)
    fix_block(3)

    def contribution(k):
        att, fix = (att_st, fx_st) if k == 3 else (att_r, fx_r)
        side = pl.multiple_of(256 * ((core + RELATION[k]) % 2), 256)
        for h in range(HEADS):
            feats, here = pl.ds(h * HEAD, HEAD), pl.ds(side + 128 * (h // 2), 128)
            new = fix[k, h // 2 * HEAD:(h // 2 + 1) * HEAD, :]
            mine = half_lane if h % 2 == 0 else jnp.logical_not(half_lane)
            att[k, feats, here] = jnp.where(mine, new, att[k, feats, here])
        turned = att[k].astype(F32).T
        for m in range(64):
            for t in range(2):
                pp[0, t, pl.ds(8 * (m % 8) + m // 8, 8, stride=64), :] = turned[8 * m:8 * m + 8, 128 * t:128 * t + 128]
        rows = jnp.concatenate([pp[0, 0], pp[0, 1]], axis=1).astype(BF16)
        return rows

    def out_copy(q):
        here = pl.ds(q * 128, 128)
        return pltpu.make_async_copy(total.at[here], out_ref.at[here], out_sem.at[q])

    for n, k in enumerate((3, 2, 0, 1)):
        if k < 3:
            arrived(*[f"b{4 * k + h}" for h in range(HEADS)], f"f{k}")
        if k == 1:
            arrived("w2")
        if k == 2:
            arrived("wc")
        turned = contribution(k)
        for q in range(4):
            here = pl.ds(q * 128, 128)
            product = dot(turned[q * 128:(q + 1) * 128], wo[k]).astype(BF16).astype(F32)
            if n == 0:
                total[here, :] = product
            else:
                total[here, :] += product
            if n == 3:
                out_copy(q).start()
    for q in range(4):
        out_copy(q).wait()
    for name in COPIES:
        copy(name).wait_send()


def on_device(tokens, norm_gain, w_qkv, w_out):
    vm = pltpu.VMEM
    return pl.pallas_call(
        kernel,
        out_shape=jax.ShapeDtypeStruct((ROWS, 1024), F32),
        in_specs=[
            pl.BlockSpec(memory_space=pl.ANY),
            pl.BlockSpec(memory_space=pltpu.VMEM),
            pl.BlockSpec(memory_space=pl.ANY),
            pl.BlockSpec(memory_space=pl.ANY),
        ],
        out_specs=pl.BlockSpec(memory_space=pl.ANY),
        scratch_shapes=[
            vm((4, ROWS, 1024), BF16),
            vm((3, 1024, FEATS), BF16),
            vm((2, ROWS, 1024), BF16),
            vm((2, 6, ROWS, 128), F32),
            vm((HEADS, KEYS, 128), BF16),
            vm((HEADS, 128, KEYS), BF16),
            vm((HEADS, 80, KEYS), BF16),
            vm((4, 4, HEADS, 64, 128), BF16),
            vm((2, 256, FEATS), BF16),
            vm((HEADS, 128, 512), BF16),
            vm((HEADS, 80, 1024), BF16),
            vm((HEADS, 32, 128), F32),
            vm((4, 4, HEADS, 32, 128), BF16),
            vm((32, FEATS), F32),
            vm((4, 32, FEATS), BF16),
            vm((HEADS, 128, 128), BF16),
            vm((HEADS, 80, 512), BF16),
            vm((HEADS, 72, 256), F32),
            vm((HEADS, 72, 256), F32),
            vm((HEADS, 72, 256), F32),
            vm((4, 72, 128), F32),
            vm((3, 72, 128), F32),
            vm((4, HEADS, 72, ROWS), F32),
            vm((4, FEATS, ROWS), BF16),
            vm((3, FEATS, ROWS), BF16),
            vm((4, 128, 128), BF16),
            vm((3, 128, 128), BF16),
            vm((4, FEATS, 1024), BF16),
            vm((KEYS, ROWS), F32),
            vm((KEYS, ROWS), F32),
            vm((1024, ROWS), F32),
            vm((HEADS, 72, 256), F32),
            pltpu.SemaphoreType.DMA((len(COPIES),)),
            pltpu.SemaphoreType.DMA((len(COPIES),)),
            pltpu.SemaphoreType.DMA((4,)),
            pltpu.SemaphoreType.DMA((3,)),
            pltpu.SemaphoreType.DMA,
            vm((ROWS, 1024), F32),
            pltpu.SemaphoreType.DMA((4,)),
        ],
        compiler_params=pltpu.CompilerParams(
            collective_id=0, has_side_effects=True, vmem_limit_bytes=56 * 1024 * 1024
        ),
    )(tokens, norm_gain.reshape(1, 1024), jnp.transpose(w_qkv, (1, 0, 2)), w_out)


def solution(mesh):
    return jax.shard_map(
        on_device,
        mesh=mesh,
        in_specs=(P("seq", None), P(), P(None, None, "head"), P("head", None)),
        out_specs=P(("seq", "head"), None),
        check_vma=False,
    )
```
